32 devices in a mesh: dp: 4 (over y, x), grid: 8 (over z, core).
Axes of the slice: x: 2, y: 2, z: 4, core: 2. Of those that a mesh axis runs over, the one named last changes fastest.
Arguments:
- intensities: bfloat16 [2048, 32, 128], P(('dp', 'grid')), may hold values from -6 to 6
- gridding: bfloat16 [2048, 32, 2048], P(('dp', 'grid')), may hold values from -0.0625 to 0.0625
- dest_slab: int32 [2048, 1], P(('dp', 'grid')), may hold values from 0 to 7; in each aligned block of 64 rows (0 to 63, 64 to 127, ...) at most 16 rows name the same one
- spectral_weights: float32 [4, 128, 128, 128], P('dp', None, 'grid'), may hold values from 0.05 to 2
Outputs:
- solution_field: float32 [128, 128, 128], P('grid')
- residual: float32 [128, 128, 128], P('grid')
The draws below stay inside these ranges and needn't reach their ends.
Inputs may be any that keep to these rules, and one draw needn't show every extreme that they name: `dest_slab`: at most 16 of one device's 64 snapshots name the same slab, and in every draw some device has exactly 16 that name one slab.
All inputs are finite; a program needn't handle non-finite values.
Results may differ from the reference program's by a relative error of at most 0.0003.
Values may be sent and summed in bfloat16 or wider, within the bound.
A program may use at most 128 MiB of HBM per device.

```python
import math
import jax
import jax.numpy as jnp
import numpy as np
from jax import lax

M = 128
R = 32
NENT = 64
ITERS = 8
SLAB = 16
CAP = 16
ENTRIES = 2048
GROUPS = 4
N_DP = 4
N_GRID = 8


def block_scale(rng, shape, pieces, least, high):
    loudness = 1.0
    for axis_at, blocks in pieces:
        draws = jax.random.uniform(jax.random.fold_in(jax.random.fold_in(rng, 6), axis_at), (blocks,), jnp.float32, least / len(pieces), high / len(pieces))
        loudness = loudness * jnp.repeat(jnp.exp(draws), shape[axis_at] // blocks).reshape((-1,) + (1,) * (len(shape) - 1 - axis_at))
    return loudness


def deal_out(own_key, own, number, rows, count, top, most, slope):
    sequence = jax.random.permutation(own_key, count)
    heavy_load, common = portions_of(count, rows * top, most, slope, True), portions_of(count, rows * top, most, slope, False)
    places = jnp.arange(count)

    def named(lengths, turn):
        used = int((lengths > 0).sum())
        fixed = max(1, used // 4)
        moved = fixed + (places - fixed + turn * (used - fixed)) % max(1, count - fixed)
        return jnp.zeros((count,), jnp.int32).at[sequence[jnp.where(places < fixed, places, moved)]].set(jnp.asarray(lengths, jnp.int32))

    lengths = jnp.where(number % 4 == 0, named(heavy_load, number // 4), named(common, number - number // 4 - 1))
    mixed = jax.random.permutation(jax.random.fold_in(own, 3), count)
    source_of, taker = mixed[0:count // 2 * 2:2], mixed[1:count // 2 * 2:2]
    margin = jnp.minimum(lengths[source_of] - 1, most - lengths[taker]) // 2
    margin = jnp.where((source_of == sequence[0]) | (taker == sequence[0]) | (lengths[taker] == 0), 0, jnp.maximum(margin, 0))
    moved = jax.random.randint(jax.random.fold_in(own, 4), (count // 2,), 0, 1 << 20) % (margin + 1)
    lengths = lengths.at[source_of].add(-moved).at[taker].add(moved)
    labels = jnp.searchsorted(jnp.cumsum(lengths), jnp.arange(rows * top), side="right").astype(jnp.int32)
    table = labels.reshape(top, rows).T
    table = table[jax.random.permutation(jax.random.fold_in(own, 1), rows)]
    turn = jax.random.randint(jax.random.fold_in(own, 2), (rows, 1), 0, top)
    return jnp.take_along_axis(table, (jnp.arange(top)[None, :] + turn) % top, axis=1)


def portions_of(amount, total, limit, skew, full):
    weights = [(1 << 20) // math.isqrt(grade ** skew) + 1 for grade in range(1, amount + 1)]
    largest = limit if full else min(limit, max(-(-total // amount), total * weights[0] // sum(weights)))
    least = 1 if total - largest >= amount - 1 else 0
    holding, rest = [largest] + [least] * (amount - 1), total - largest - least * (amount - 1)
    while rest > 0:
        candidates = [i for i in range(1, amount) if holding[i] < largest] or [i for i in range(1, amount) if holding[i] < limit]
        mass, left = sum([weights[i] for i in candidates]), rest
        for i in candidates:
            extra = min(limit - holding[i], max(1, left * weights[i] // mass), rest)
            holding[i] = holding[i] + extra
            rest = rest - extra
    return np.array(holding)


def scatter_about(own_key, shape, scale, bound, cuts=(), kind=jnp.bfloat16):
    array = scale * jax.random.normal(own_key, shape, jnp.float32)
    if cuts:
        array = array * block_scale(own_key, shape, cuts, -0.22, 0.18)
    return jnp.clip(array, -bound, bound).astype(kind)


def setup_inputs(seed: int = 0) -> dict:
    key_of = jax.random.split(jax.random.key(seed), 5)
    intensities = scatter_about(key_of[0], (ENTRIES, R, M), 1.0, 6.0, ((0, 32),))
    gridding = scatter_about(key_of[1], (ENTRIES, R, SLAB * M), (R * N_DP * NENT) ** -0.5, 0.0625, ((0, 32),))
    dest_slab_keys = jax.random.split(jax.random.fold_in(key_of[2], 1), ENTRIES // NENT)
    dest_slab_turns = jax.random.permutation(jax.random.fold_in(key_of[2], 3), ENTRIES // NENT)
    dest_slab = jax.vmap(lambda own, number: deal_out(jax.random.fold_in(key_of[2], 2), own, number, NENT, N_GRID, 1, CAP, 2))(dest_slab_keys, dest_slab_turns).reshape((ENTRIES, 1))
    spectral_weights = jnp.clip(jnp.exp(math.log(2.0) - 3.6888794 * jax.random.uniform(key_of[3], (GROUPS, M, M, M), jnp.float32) ** block_scale(key_of[3], (GROUPS, M, M, M), ((0, 4), (2, 8)), -0.2, 0.2)), 0.05, 2.0)
    return dict(intensities=intensities, gridding=gridding, dest_slab=dest_slab, spectral_weights=spectral_weights)


def operate(field, weight_sum):
    spectrum = jnp.fft.fftn(field)
    return jnp.real(jnp.fft.ifftn(weight_sum * spectrum)).astype(field.dtype)


def reference(intensities, gridding, dest_slab, spectral_weights):
    blocks = ENTRIES // NENT
    vals = intensities.reshape(blocks, NENT, R, M)
    mats = gridding.reshape(blocks, NENT, R, SLAB * M)
    targets = dest_slab.reshape(blocks, NENT).astype(jnp.int32)

    def add_block(total, block):
        block_vals, block_mats, block_dest = block
        contrib = jnp.einsum("krq,krz->kqz", block_mats.astype(jnp.float32), block_vals.astype(jnp.float32))
        return total.at[block_dest].add(contrib), None

    start = jnp.zeros((N_GRID, SLAB * M, M), jnp.float32)
    total, _ = lax.scan(add_block, start, (vals, mats, targets))
    right_side = total.reshape(M, M, M)
    weight_sum = jnp.sum(spectral_weights, axis=0)
    solution_field = jnp.zeros_like(right_side)
    residual, direction = right_side, right_side
    norm_now = jnp.sum(residual * residual)
    for step in range(ITERS):
        image = operate(direction, weight_sum)
        alpha = norm_now / jnp.sum(direction * image)
        solution_field = solution_field + alpha * direction
        residual = residual - alpha * image
        norm_next = jnp.sum(residual * residual)
        direction = residual + (norm_next / norm_now) * direction
        norm_now = norm_next
    return solution_field, residual
```

```python
import functools
import math

import jax
import jax.numpy as jnp
import numpy as np
from jax import lax
from jax.experimental import pallas as pl
from jax.experimental.pallas import tpu as pltpu
from jax.sharding import PartitionSpec as P

ITERS = 8
HIGH = lax.Precision.HIGHEST


def half_size(size, ndp):
    return -(-(size // 2 + 1) // ndp)


def angles(rows, columns, size):
    return 2.0 * np.pi * ((rows[:, None] * columns[None, :]) % size) / size


def counts(size, kept):
    index = np.arange(kept)
    count = np.where((index == 0) | (2 * index == size), 1.0, 2.0)
    return np.where(2 * index > size, 0.0, count)


def first_table(size, ndp):
    each = half_size(size, ndp)
    index = np.arange(each * ndp)
    angle = angles(index, np.arange(size), size)
    table = np.stack([np.cos(angle), -np.sin(angle)])
    table = table * (counts(size, each * ndp) > 0)[None, :, None]
    return table.reshape(2, ndp, each, size).transpose(1, 0, 2, 3).astype(np.float32)


def last_table(size, ndp):
    each = half_size(size, ndp)
    index = np.arange(each * ndp)
    angle = angles(index, np.arange(size), size)
    table = np.stack([np.cos(angle), -np.sin(angle)])
    table = table * counts(size, each * ndp)[None, :, None] / float(size) ** 3
    return table.reshape(2, ndp, each, size).transpose(1, 0, 2, 3).astype(np.float32)


def complex_table(size, sign):
    angle = angles(np.arange(size), np.arange(size), size)
    cos, sin = np.cos(angle), sign * np.sin(angle)
    return np.stack([np.stack([cos, sin], 1), np.stack([-sin, cos], 1)]).astype(np.float32)


def along(form, field, table):
    return jnp.einsum(form, field, table, precision=HIGH)


def shared_sum(row, axis, count, inbox, outbox, send_sem, recv_sem, turn):
    me = lax.axis_index(axis)
    outbox[turn] = row
    copies = []
    for step in range(1, count):
        peer = lax.rem(me + step, count)
        copy = pltpu.make_async_remote_copy(
            src_ref=outbox.at[turn],
            dst_ref=inbox.at[turn, step - 1],
            send_sem=send_sem.at[turn, step - 1],
            recv_sem=recv_sem.at[turn, step - 1],
            device_id={axis: peer},
            device_id_type=pl.DeviceIdType.MESH,
        )
        copy.start()
        copies.append(copy)
    total = row
    for step in range(1, count):
        copies[step - 1].wait_recv()
        total = total + inbox[turn, step - 1]
    for copy in copies:
        copy.wait_send()
    return total


def scalar_kernel(ngrid, ndp, power_ref, weight_ref, rho_ref, sigma_ref,
                  delta_ref, grid_in, grid_out, dp_in, dp_out, gs, gr, ds, dr):
    me_grid, me_dp = lax.axis_index("grid"), lax.axis_index("dp")
    barrier = pltpu.get_barrier_semaphore()
    for step in range(1, ngrid):
        pl.semaphore_signal(barrier, inc=1, device_id={"grid": lax.rem(me_grid + step, ngrid)},
                            device_id_type=pl.DeviceIdType.MESH)
    for step in range(1, ndp):
        pl.semaphore_signal(barrier, inc=1, device_id={"dp": lax.rem(me_dp + step, ndp)},
                            device_id_type=pl.DeviceIdType.MESH)
    pl.semaphore_wait(barrier, ngrid + ndp - 2)
    lane = lax.broadcasted_iota(jnp.int32, (1, 128), 1)
    power, weight = power_ref[...], weight_ref[...]
    rho_ref[...] = jnp.ones_like(power)
    sigma_ref[...] = jnp.zeros_like(power)
    delta_ref[...] = jnp.zeros_like(power)

    def step(index, carry):
        norm_before, alpha_before = carry
        turn = lax.rem(index, 2)
        rho = rho_ref[...]
        square = rho * rho * power
        norm = jnp.sum(square)
        product = jnp.sum(square * weight)
        row = jnp.where(lane == 0, norm, jnp.where(lane == 1, product, 0.0))
        row = shared_sum(row, "grid", ngrid, grid_in, grid_out, gs, gr, turn)
        row = shared_sum(row, "dp", ndp, dp_in, dp_out, ds, dr, turn)
        norm = jnp.sum(jnp.where(lane == 0, row, 0.0), axis=1, keepdims=True)
        product = jnp.sum(jnp.where(lane == 1, row, 0.0), axis=1, keepdims=True)
        ratio = norm / norm_before
        first = jnp.full((1, 1), index, jnp.int32) == 0
        ratio = jnp.where(first, 0.0, ratio)
        product = product - jnp.where(first, 0.0, ratio * norm / alpha_before)
        alpha = norm / product
        delta = rho + ratio * delta_ref[...]
        delta_ref[...] = delta
        sigma_ref[...] = sigma_ref[...] + alpha * delta
        rho_ref[...] = rho - alpha * (weight * delta)
        return norm, alpha

    one = jnp.ones((1, 1), jnp.float32)
    lax.fori_loop(0, ITERS, step, (one, one))


def multipliers(power, weight):
    ngrid, ndp = lax.axis_size("grid"), lax.axis_size("dp")
    shape = jax.ShapeDtypeStruct(power.shape, jnp.float32)
    vmem = pl.BlockSpec(memory_space=pltpu.VMEM)
    dma = pltpu.SemaphoreType.DMA
    return pl.pallas_call(
        functools.partial(scalar_kernel, ngrid, ndp),
        out_shape=(shape, shape),
        in_specs=[vmem, vmem],
        out_specs=(vmem, vmem),
        scratch_shapes=[
            pltpu.VMEM(power.shape, jnp.float32),
            pltpu.VMEM((2, ngrid - 1, 1, 128), jnp.float32),
            pltpu.VMEM((2, 1, 128), jnp.float32),
            pltpu.VMEM((2, ndp - 1, 1, 128), jnp.float32),
            pltpu.VMEM((2, 1, 128), jnp.float32),
            dma((2, ngrid - 1)), dma((2, ngrid - 1)), dma((2, ndp - 1)), dma((2, ndp - 1)),
        ],
        compiler_params=pltpu.CompilerParams(collective_id=0, has_side_effects=True),
    )(power, weight)


def spectral_weight(weights, ngrid, ndp, each, size):
    turned = jnp.transpose(weights, (2, 1, 0))
    kept = each * ndp
    front = turned[:kept]
    back = jnp.roll(jnp.flip(turned, (0, 2)), (1, 1), (0, 2))[:kept]
    both = jnp.stack([front, back])
    both = both.reshape(2, ndp, each, both.shape[2], size).transpose(1, 0, 2, 3, 4)
    both = lax.psum_scatter(both, "dp", scatter_dimension=0, tiled=True)[0]
    front, back = both[0], both[1]
    edge = lax.ppermute(back[:, :1], "grid", [(g, (ngrid - g) % ngrid) for g in range(ngrid)])
    rest = lax.ppermute(back[:, 1:], "grid", [(g, ngrid - 1 - g) for g in range(ngrid)])
    back = jnp.concatenate([edge, jnp.flip(rest, 1)], axis=1)
    return 0.5 * (front + back)


def gridded(intensities, gridding, dest_slab, ngrid, ndp, each):
    nent, rows, size = intensities.shape
    slab_rows = gridding.shape[2]
    planes = slab_rows // size
    member = dest_slab == jnp.arange(ngrid, dtype=jnp.int32)[None, :]
    values = jnp.where(member[:, None, :, None], intensities[:, :, None, :], 0)
    values = values.reshape(nent * rows, ngrid * size)
    matrix = gridding.reshape(nent * rows, slab_rows)
    product = lax.dot_general(
        values, matrix, (((0,), (0,)), ((), ())), preferred_element_type=jnp.float32
    ).reshape(ngrid, size, slab_rows)
    table = first_table(size, ndp).reshape(ndp * 2 * each, size)
    spread = jnp.stack([
        lax.dot_general(jnp.asarray(table), product[s], (((1,), (0,)), ((), ())), precision=HIGH)
        for s in range(ngrid)
    ], axis=1).reshape(ndp, 2 * each, ngrid, slab_rows)
    part = lax.psum_scatter(spread, "dp", scatter_dimension=0, tiled=True)[0]
    part = jnp.transpose(part, (1, 0, 2))
    part = lax.psum_scatter(part, "grid", scatter_dimension=0, tiled=True)[0]
    return part.reshape(2, each, planes, size)


def body(intensities, gridding, dest_slab, spectral_weights):
    ngrid = lax.axis_size("grid")
    ndp = lax.axis_size("dp")
    nent, rows, size = intensities.shape
    each = half_size(size, ndp)
    weight = spectral_weight(spectral_weights[0], ngrid, ndp, each, size)
    part = gridded(intensities, gridding, dest_slab, ngrid, ndp, each)
    ahead, back = complex_table(size, -1.0), complex_table(size, 1.0)
    rows_done = along("ckxy,cydj->dkxj", part, ahead)
    columns = lax.all_to_all(rows_done, "grid", split_axis=3, concat_axis=2, tiled=True)
    spectrum = along("ckxj,cxdm->dkjm", columns, ahead)
    share = lax.dynamic_slice_in_dim(
        jnp.asarray(counts(size, each * ndp), jnp.float32), lax.axis_index("dp") * each, each
    )
    power = share[:, None, None] * (spectrum[0] * spectrum[0] + spectrum[1] * spectrum[1])
    rho, sigma = multipliers(power.reshape(-1, size), weight.reshape(-1, size))
    fields = jnp.stack([sigma, rho]).reshape((2, 1) + power.shape) * spectrum[None]
    columns = along("fckjm,cmdx->fdkxj", fields, back)
    planes = lax.all_to_all(columns, "grid", split_axis=3, concat_axis=4, tiled=True)
    planes = along("fckxj,cjdy->fdkxy", planes, back)
    whole = lax.all_gather(planes, "dp", axis=0, tiled=False)
    table = last_table(size, ndp)
    return tuple(along("dckxy,dckz->xyz", whole[:, f], table) for f in range(2))


def solution(mesh):
    return jax.shard_map(
        body,
        mesh=mesh,
        in_specs=(
            P(("dp", "grid"), None, None),
            P(("dp", "grid"), None, None),
            P(("dp", "grid"), None),
            P("dp", None, "grid", None),
        ),
        out_specs=(P("grid", None, None), P("grid", None, None)),
        check_vma=False,
    )
```

```python
import functools
import math

import jax
import jax.numpy as jnp
import numpy as np
from jax import lax
from jax.experimental import pallas as pl
from jax.experimental.pallas import tpu as pltpu
from jax.sharding import PartitionSpec as P

ITERS = 8
HIGH = lax.Precision.HIGHEST


def angles(rows, columns, size):
    return 2.0 * np.pi * ((rows[:, None] * columns[None, :]) % size) / size


def slot_index(size, ndp):
    each = size // 2 // ndp
    index = np.full((ndp, each + 1), size // 2)
    index[:, :each] = np.arange(size // 2).reshape(ndp, each)
    return index


def counts(size, ndp):
    index = slot_index(size, ndp)
    count = np.where(index == 0, 1.0, 2.0)
    count[:, -1] = 0.0
    count[0, -1] = 1.0
    return count.astype(np.float32)


def first_table(size, ndp):
    angle = angles(np.arange(size // 2), np.arange(size), size)
    real, imag = np.cos(angle), -np.sin(angle)
    imag[0] = np.cos(np.pi * np.arange(size))
    table = np.stack([real, imag]).reshape(2, ndp, -1, size)
    return table.transpose(1, 0, 2, 3).reshape(size, size).astype(np.float32)


def last_table(size, ndp):
    index = slot_index(size, ndp)
    angle = angles(index.reshape(-1), np.arange(size), size).reshape(index.shape + (size,))
    table = np.stack([np.cos(angle), -np.sin(angle)], 1)
    return (table * counts(size, ndp)[:, None, :, None] / float(size) ** 3).astype(np.float32)


def complex_table(size, sign):
    angle = angles(np.arange(size), np.arange(size), size)
    cos, sin = np.cos(angle), sign * np.sin(angle)
    return np.stack([np.stack([cos, sin], 1), np.stack([-sin, cos], 1)]).astype(np.float32)


def along(form, field, table):
    return jnp.einsum(form, field, table, precision=HIGH)


def shared_sum(row, axis, count, inbox, outbox, send_sem, recv_sem, turn):
    me = lax.axis_index(axis)
    outbox[turn] = row
    copies = []
    for step in range(1, count):
        peer = lax.rem(me + step, count)
        copy = pltpu.make_async_remote_copy(
            src_ref=outbox.at[turn],
            dst_ref=inbox.at[turn, step - 1],
            send_sem=send_sem.at[turn, step - 1],
            recv_sem=recv_sem.at[turn, step - 1],
            device_id={axis: peer},
            device_id_type=pl.DeviceIdType.MESH,
        )
        copy.start()
        copies.append(copy)
    total = row
    for step in range(1, count):
        copies[step - 1].wait_recv()
        total = total + inbox[turn, step - 1]
    for copy in copies:
        copy.wait_send()
    return total


def scalar_kernel(ngrid, ndp, power_ref, weight_ref, rho_ref, sigma_ref,
                  delta_ref, grid_in, grid_out, dp_in, dp_out, gs, gr, ds, dr):
    me_grid, me_dp = lax.axis_index("grid"), lax.axis_index("dp")
    barrier = pltpu.get_barrier_semaphore()
    for step in range(1, ngrid):
        pl.semaphore_signal(barrier, inc=1, device_id={"grid": lax.rem(me_grid + step, ngrid)},
                            device_id_type=pl.DeviceIdType.MESH)
    for step in range(1, ndp):
        pl.semaphore_signal(barrier, inc=1, device_id={"dp": lax.rem(me_dp + step, ndp)},
                            device_id_type=pl.DeviceIdType.MESH)
    pl.semaphore_wait(barrier, ngrid + ndp - 2)
    lane = lax.broadcasted_iota(jnp.int32, (1, 128), 1)
    power, weight = power_ref[...], weight_ref[...]
    rho_ref[...] = jnp.ones_like(power)
    sigma_ref[...] = jnp.zeros_like(power)
    delta_ref[...] = jnp.zeros_like(power)

    def step(index, carry):
        norm_before, alpha_before = carry
        turn = lax.rem(index, 2)
        rho = rho_ref[...]
        square = rho * rho * power
        norm = jnp.sum(square)
        product = jnp.sum(square * weight)
        row = jnp.where(lane == 0, norm, jnp.where(lane == 1, product, 0.0))
        row = shared_sum(row, "grid", ngrid, grid_in, grid_out, gs, gr, turn)
        row = shared_sum(row, "dp", ndp, dp_in, dp_out, ds, dr, turn)
        norm = jnp.sum(jnp.where(lane == 0, row, 0.0), axis=1, keepdims=True)
        product = jnp.sum(jnp.where(lane == 1, row, 0.0), axis=1, keepdims=True)
        ratio = norm / norm_before
        first = jnp.full((1, 1), index, jnp.int32) == 0
        ratio = jnp.where(first, 0.0, ratio)
        product = product - jnp.where(first, 0.0, ratio * norm / alpha_before)
        alpha = norm / product
        delta = rho + ratio * delta_ref[...]
        delta_ref[...] = delta
        sigma_ref[...] = sigma_ref[...] + alpha * delta
        rho_ref[...] = rho - alpha * (weight * delta)
        return norm, alpha

    one = jnp.ones((1, 1), jnp.float32)
    lax.fori_loop(0, ITERS, step, (one, one))


def multipliers(power, weight):
    ngrid, ndp = lax.axis_size("grid"), lax.axis_size("dp")
    shape = jax.ShapeDtypeStruct(power.shape, jnp.float32)
    vmem = pl.BlockSpec(memory_space=pltpu.VMEM)
    dma = pltpu.SemaphoreType.DMA
    return pl.pallas_call(
        functools.partial(scalar_kernel, ngrid, ndp),
        out_shape=(shape, shape),
        in_specs=[vmem, vmem],
        out_specs=(vmem, vmem),
        scratch_shapes=[
            pltpu.VMEM(power.shape, jnp.float32),
            pltpu.VMEM((2, ngrid - 1, 1, 128), jnp.float32),
            pltpu.VMEM((2, 1, 128), jnp.float32),
            pltpu.VMEM((2, ndp - 1, 1, 128), jnp.float32),
            pltpu.VMEM((2, 1, 128), jnp.float32),
            dma((2, ngrid - 1)), dma((2, ngrid - 1)), dma((2, ndp - 1)), dma((2, ndp - 1)),
        ],
        compiler_params=pltpu.CompilerParams(collective_id=0, has_side_effects=True),
    )(power, weight)


def grid_kernel(ngrid, ndp, size, values_ref, matrix_ref, table_ref, weight_ref,
                part_ref, total_ref, own, sibling, pair_in, dp_in, ready, group_in, weight_in,
                pair_s, pair_r, dp_s, dp_r, group_s, group_r, weight_s, weight_r):
    grid, dp = lax.axis_index("grid"), lax.axis_index("dp")
    groups = ngrid // 2
    core = lax.rem(grid, 2)
    group = grid // 2
    other = 2 * group + 1 - core
    mesh_id = pl.DeviceIdType.MESH
    barrier = pltpu.get_barrier_semaphore()
    pl.semaphore_signal(barrier, inc=1, device_id={"grid": other}, device_id_type=mesh_id)
    for step in range(1, groups):
        peer = 2 * lax.rem(group + step, groups) + core
        pl.semaphore_signal(barrier, inc=1, device_id={"grid": peer}, device_id_type=mesh_id)
    for step in range(1, ndp):
        pl.semaphore_signal(barrier, inc=1, device_id={"dp": lax.rem(dp + step, ndp)},
                            device_id_type=mesh_id)
    pl.semaphore_wait(barrier, groups + ndp - 1)

    weight_copies = []
    for step in range(1, ndp):
        peer = lax.rem(dp + step, ndp)
        copy = pltpu.make_async_remote_copy(
            src_ref=weight_ref.at[peer], dst_ref=weight_in.at[step - 1],
            send_sem=weight_s.at[step - 1], recv_sem=weight_r.at[step - 1],
            device_id={"dp": peer}, device_id_type=mesh_id)
        copy.start()
        weight_copies.append(copy)

    columns = matrix_ref.shape[1]
    tile = math.gcd(columns, 512)
    rows = size // ndp

    def compute(step):
        chunk = lax.rem(group + 1 + step, groups)

        @pl.loop(0, columns // tile)
        def _(index):
            at = pl.ds(pl.multiple_of(index * tile, tile), tile)
            product = jnp.dot(values_ref[chunk], matrix_ref[:, at],
                              preferred_element_type=jnp.float32)
            for half, buffer in enumerate((own, sibling)):
                turned = jnp.dot(table_ref[...], product[half * size:(half + 1) * size],
                                 precision=HIGH, preferred_element_type=jnp.float32)
                buffer[step, :, :, at] = turned.reshape(ndp, rows, tile)

    def send_pair(step):
        copy = pltpu.make_async_remote_copy(
            src_ref=sibling.at[step], dst_ref=pair_in.at[step],
            send_sem=pair_s.at[step], recv_sem=pair_r.at[step],
            device_id={"grid": other}, device_id_type=mesh_id)
        copy.start()
        return [copy]

    def send_dp(step):
        copies = []
        for turn in range(1, ndp):
            peer = lax.rem(dp + turn, ndp)
            own[step, peer] = own[step, peer] + pair_in[step, peer]
            copy = pltpu.make_async_remote_copy(
                src_ref=own.at[step, peer], dst_ref=dp_in.at[step, turn - 1],
                send_sem=dp_s.at[step, turn - 1], recv_sem=dp_r.at[step, turn - 1],
                device_id={"dp": peer}, device_id_type=mesh_id)
            copy.start()
            copies.append(copy)
        ready[step] = own[step, dp] + pair_in[step, dp]
        return copies

    def send_group(step):
        total = ready[step]
        for turn in range(ndp - 1):
            total = total + dp_in[step, turn]
        ready[step] = total
        if step == groups - 1:
            return []
        peer = 2 * lax.rem(group + 1 + step, groups) + core
        copy = pltpu.make_async_remote_copy(
            src_ref=ready.at[step], dst_ref=group_in.at[step],
            send_sem=group_s.at[step], recv_sem=group_r.at[step],
            device_id={"grid": peer}, device_id_type=mesh_id)
        copy.start()
        return [copy]

    pair_copies, dp_copies, group_copies = [], [], []
    for step in range(groups + 2):
        if step < groups:
            compute(step)
            pair_copies.append(send_pair(step))
        if 1 <= step <= groups:
            for copy in pair_copies[step - 1]:
                copy.wait_recv()
            dp_copies.append(send_dp(step - 1))
        if step >= 2:
            for copy in dp_copies[step - 2]:
                copy.wait_recv()
            group_copies.append(send_group(step - 2))
    for copy in weight_copies:
        copy.wait_recv()
    total = weight_ref[dp]
    for step in range(ndp - 1):
        total = total + weight_in[step]
    total_ref[...] = total
    part = ready[groups - 1]
    for step in range(groups - 1):
        for copy in group_copies[step]:
            copy.wait_recv()
        part = part + group_in[step]
    part_ref[...] = part
    for copies in pair_copies + dp_copies + group_copies + [weight_copies]:
        for copy in copies:
            copy.wait_send()


def gridded(intensities, gridding, dest_slab, weights, ngrid, ndp):
    nent, rows, size = intensities.shape
    slab_rows = gridding.shape[2]
    core = lax.axis_index("grid") % 2
    groups, share = ngrid // 2, size // ndp
    slabs = 2 * np.arange(groups)[:, None] + jnp.stack([core, 1 - core])[None, :]
    target = jnp.repeat(dest_slab[:, 0], rows)
    member = target[None, None, :] == slabs[:, :, None]
    turned = intensities.reshape(nent * rows, size).T
    values = jnp.where(member[:, :, None, :], turned[None, None], 0)
    values = values.reshape(groups, 2 * size, nent * rows)
    matrix = gridding.reshape(nent * rows, slab_rows)
    vmem = pl.BlockSpec(memory_space=pltpu.VMEM)
    dma = pltpu.SemaphoreType.DMA
    f32 = jnp.float32
    return pl.pallas_call(
        functools.partial(grid_kernel, ngrid, ndp, size),
        out_shape=(jax.ShapeDtypeStruct((share, slab_rows), f32),
                   jax.ShapeDtypeStruct(weights.shape[1:], f32)),
        in_specs=[vmem] * 4,
        out_specs=(vmem, vmem),
        scratch_shapes=[
            pltpu.VMEM((groups, ndp, share, slab_rows), f32),
            pltpu.VMEM((groups, ndp, share, slab_rows), f32),
            pltpu.VMEM((groups, ndp, share, slab_rows), f32),
            pltpu.VMEM((groups, ndp - 1, share, slab_rows), f32),
            pltpu.VMEM((groups, share, slab_rows), f32),
            pltpu.VMEM((groups - 1, share, slab_rows), f32),
            pltpu.VMEM((ndp - 1,) + weights.shape[1:], f32),
            dma((groups,)), dma((groups,)), dma((groups, ndp - 1)), dma((groups, ndp - 1)),
            dma((groups - 1,)), dma((groups - 1,)), dma((ndp - 1,)), dma((ndp - 1,)),
        ],
        compiler_params=pltpu.CompilerParams(
            collective_id=1, has_side_effects=True, vmem_limit_bytes=52 * 2 ** 20),
    )(values, matrix, jnp.asarray(first_table(size, ndp)), weights)


def mirrored(weights, ndp):
    size = weights.shape[0]
    turned = jnp.transpose(weights, (2, 1, 0))
    flipped = jnp.roll(jnp.flip(turned, (0, 2)), (1, 1), (0, 2))
    each, half = size // 2 // ndp, size // 2
    shares = [
        jnp.concatenate([field[d * each:(d + 1) * each], field[half:half + 1]])
        for d in range(ndp) for field in (turned, flipped)
    ]
    return jnp.stack(shares).reshape(ndp, -1, size)


def spectral_weight(both, ngrid):
    front, back = both[0], both[1]
    edge = lax.ppermute(back[:, :1], "grid", [(g, (ngrid - g) % ngrid) for g in range(ngrid)])
    rest = lax.ppermute(back[:, 1:], "grid", [(g, ngrid - 1 - g) for g in range(ngrid)])
    back = jnp.concatenate([edge, jnp.flip(rest, 1)], axis=1)
    return 0.5 * (front + back)


def unpacked(part, planes, size, ndp):
    part = part.reshape(2, -1, planes, size)
    lead = lax.axis_index("dp") == 0
    real, imag, zero = part[0], part[1], jnp.zeros_like(part[1, :1])
    real = jnp.concatenate([real, jnp.where(lead, imag[:1], zero)])
    imag = jnp.concatenate([jnp.where(lead, zero, imag[:1]), imag[1:], zero])
    return jnp.stack([real, imag])


def body(intensities, gridding, dest_slab, spectral_weights):
    ngrid = lax.axis_size("grid")
    ndp = lax.axis_size("dp")
    size = intensities.shape[2]
    planes = gridding.shape[2] // size
    part, both = gridded(
        intensities, gridding, dest_slab, mirrored(spectral_weights[0], ndp), ngrid, ndp)
    weight = spectral_weight(both.reshape(2, -1, spectral_weights.shape[2], size), ngrid)
    part = unpacked(part, planes, size, ndp)
    ahead, back = complex_table(size, -1.0), complex_table(size, 1.0)
    rows_done = along("ckxy,cydj->dkxj", part, ahead)
    columns = lax.all_to_all(rows_done, "grid", split_axis=3, concat_axis=2, tiled=True)
    spectrum = along("ckxj,cxdm->dkjm", columns, ahead)
    share = lax.dynamic_index_in_dim(
        jnp.asarray(counts(size, ndp)), lax.axis_index("dp"), keepdims=False)
    power = share[:, None, None] * (spectrum[0] * spectrum[0] + spectrum[1] * spectrum[1])
    rho, sigma = multipliers(power.reshape(-1, size), weight.reshape(-1, size))
    fields = jnp.stack([sigma, rho]).reshape((2, 1) + power.shape) * spectrum[None]
    columns = along("fckjm,cmdx->fdkxj", fields, back)
    planes = lax.all_to_all(columns, "grid", split_axis=3, concat_axis=4, tiled=True)
    planes = along("fckxj,cjdy->fdkxy", planes, back)
    whole = lax.all_gather(planes, "dp", axis=0, tiled=False)
    table = last_table(size, ndp)
    return tuple(along("dckxy,dckz->xyz", whole[:, f], table) for f in range(2))


def solution(mesh):
    return jax.shard_map(
        body,
        mesh=mesh,
        in_specs=(
            P(("dp", "grid"), None, None),
            P(("dp", "grid"), None, None),
            P(("dp", "grid"), None),
            P("dp", None, "grid", None),
        ),
        out_specs=(P("grid", None, None), P("grid", None, None)),
        check_vma=False,
    )
```
